32 devices in a mesh: expert: 4 (over x, core), hidden: 8 (over z, y).
Axes of the slice: x: 2, y: 2, z: 4, core: 2. Of those that a mesh axis runs over, the one named last changes fastest.
Arguments:
- tokens: bfloat16 [64, 6144], P(('expert', 'hidden')), may hold values from -6 to 6
- routing: int32 [64, 2], P(('expert', 'hidden')), may hold values from 0 to 3, all different within a row; in each aligned block of 2 rows (0 to 1, 2 to 3, ...) at most 2 rows name the same one
- mix_weights: float32 [64, 2], P(('expert', 'hidden')), may hold values from 0.2 to 1
- gate_weight: bfloat16 [4, 6144, 16384], P('expert', None, 'hidden'), may hold values from -0.078125 to 0.078125
- up_weight: bfloat16 [4, 6144, 16384], P('expert', None, 'hidden'), may hold values from -0.078125 to 0.078125
- down_weight: bfloat16 [4, 16384, 6144], P('expert', 'hidden'), may hold values from -0.0625 to 0.0625
Outputs:
- mixed: bfloat16 [64, 6144], P(('expert', 'hidden'))
The draws below stay inside these ranges and needn't reach their ends.
Inputs may be any that keep to these rules, and one draw needn't show every extreme that they name: `routing`: each row names two different experts. Within each aligned block of 2 rows (the tokens of one device) no expert is named by more than 2 entries, and in every draw some expert is named by exactly 2 entries of some block.
All inputs are finite; a program needn't handle non-finite values.
Results may differ from the reference program's by a relative error of at most 0.0058.
Values may be sent and summed in bfloat16 or wider, within the bound.
A program may use at most 128 MiB of HBM per device.

```python
import math
import jax
import jax.numpy as jnp
import numpy as np
from jax import lax

D = 6144
FF = 16384
TOK_DEV = 2
CAP = 2
EXPERTS = 4
TOKENS = 64


def spiked(values, own_key, source, target, parts, factor):
    owner, partner = [(jnp.arange(values.shape[axis_at]) // (values.shape[axis_at] // parts)).reshape([-1 if axis == axis_at else 1 for axis in range(values.ndim)]) for axis_at in (source, target)]
    chosen = jax.random.permutation(own_key, parts)[partner]
    strong = (owner == chosen) | (owner == (partner + parts // 2) % parts)
    return jnp.where(strong, factor * values, values)


def block_levels(own_key, extent, cuts, low, largest):
    level = 1.0
    for dim, parts in cuts:
        steps = jax.random.uniform(jax.random.fold_in(jax.random.fold_in(own_key, 6), dim), (parts,), jnp.float32, low / len(cuts), largest / len(cuts))
        level = level * jnp.repeat(jnp.exp(steps), extent[dim] // parts).reshape((-1,) + (1,) * (len(extent) - 1 - dim))
    return level


def assign_block(own_key, own, number, rows, amount, top, reach, lean):
    sequence = jax.random.permutation(own_key, amount)
    crowded, common = shares(amount, rows * top, reach, lean, True), shares(amount, rows * top, reach, lean, False)
    places = jnp.arange(amount)

    def named(sizes, turn):
        used = int((sizes > 0).sum())
        fixed = max(1, used // 4)
        shifted = fixed + (places - fixed + turn * (used - fixed)) % max(1, amount - fixed)
        return jnp.zeros((amount,), jnp.int32).at[sequence[jnp.where(places < fixed, places, shifted)]].set(jnp.asarray(sizes, jnp.int32))

    sizes = jnp.where(number % 4 == 0, named(crowded, number // 4), named(common, number - number // 4 - 1))
    mixed = jax.random.permutation(jax.random.fold_in(own, 3), amount)
    giver, receiver = mixed[0:amount // 2 * 2:2], mixed[1:amount // 2 * 2:2]
    slack = jnp.minimum(sizes[giver] - 1, reach - sizes[receiver]) // 2
    slack = jnp.where((giver == sequence[0]) | (receiver == sequence[0]) | (sizes[receiver] == 0), 0, jnp.maximum(slack, 0))
    shifted = jax.random.randint(jax.random.fold_in(own, 4), (amount // 2,), 0, 1 << 20) % (slack + 1)
    sizes = sizes.at[giver].add(-shifted).at[receiver].add(shifted)
    members = jnp.searchsorted(jnp.cumsum(sizes), jnp.arange(rows * top), side="right").astype(jnp.int32)
    grid = members.reshape(top, rows).T
    grid = grid[jax.random.permutation(jax.random.fold_in(own, 1), rows)]
    turn = jax.random.randint(jax.random.fold_in(own, 2), (rows, 1), 0, top)
    return jnp.take_along_axis(grid, (jnp.arange(top)[None, :] + turn) % top, axis=1)


def shares(number_of, total, bound, skew, full):
    loads = [(1 << 20) // math.isqrt(rank ** skew) + 1 for rank in range(1, number_of + 1)]
    largest = bound if full else min(bound, max(-(-total // number_of), total * loads[0] // sum(loads)))
    least = 1 if total - largest >= number_of - 1 else 0
    holding, surplus = [largest] + [least] * (number_of - 1), total - largest - least * (number_of - 1)
    while surplus > 0:
        free = [i for i in range(1, number_of) if holding[i] < largest] or [i for i in range(1, number_of) if holding[i] < bound]
        whole, budget = sum([loads[i] for i in free]), surplus
        for i in free:
            addition = min(bound - holding[i], max(1, budget * loads[i] // whole), surplus)
            holding[i] = holding[i] + addition
            surplus = surplus - addition
    return np.array(holding)


def gaussian(key, dims, scale, most, pieces=(), kind=jnp.bfloat16):
    values = scale * jax.random.normal(key, dims, jnp.float32)
    if pieces:
        values = values * block_levels(key, dims, pieces, -0.22, 0.18)
    return jnp.clip(values, -most, most).astype(kind)


def heavy_noise(own_key, extent, width, most, pieces, heavy, kind=jnp.bfloat16):
    values = width * jax.random.normal(own_key, extent, jnp.float32)
    if pieces:
        values = values * block_levels(own_key, extent, pieces, -0.22, 0.18)
    return jnp.clip(spiked(values, jax.random.fold_in(own_key, 3), *heavy), -most, most).astype(kind)


def setup_inputs(seed: int = 0) -> dict:
    key_list = jax.random.split(jax.random.key(seed), 7)
    tokens = gaussian(key_list[0], (TOKENS, D), 1.0, 6.0, ((0, 32),))
    routing_keys = jax.random.split(jax.random.fold_in(key_list[1], 1), TOKENS // TOK_DEV)
    routing_turns = jax.random.permutation(jax.random.fold_in(key_list[1], 3), TOKENS // TOK_DEV)
    routing = jax.vmap(lambda own, number: assign_block(jax.random.fold_in(key_list[1], 2), own, number, TOK_DEV, EXPERTS, 2, CAP, 1))(routing_keys, routing_turns).reshape((TOKENS, 2))
    mix_weights = jnp.clip(0.2 + 0.8 * jax.random.uniform(key_list[2], (TOKENS, 2), jnp.float32) ** block_levels(key_list[2], (TOKENS, 2), ((0, 32),), -0.2, 0.2), 0.2, 1.0)
    gate_weight = gaussian(key_list[3], (EXPERTS, D, FF), D ** -0.5, 0.078125, ((0, 4), (2, 8)))
    up_weight = gaussian(key_list[4], (EXPERTS, D, FF), D ** -0.5, 0.078125, ((0, 4), (2, 8)))
    down_weight = heavy_noise(key_list[5], (EXPERTS, FF, D), FF ** -0.5, 0.0625, ((0, 4), (1, 8)), (1, 2, 8, 2.0))
    return {"tokens": tokens, "routing": routing, "mix_weights": mix_weights, "gate_weight": gate_weight, "up_weight": up_weight, "down_weight": down_weight}


def reference(tokens, routing, mix_weights, gate_weight, up_weight, down_weight):
    blocks = TOKENS // TOK_DEV
    entries = routing.reshape(blocks, 2 * TOK_DEV).astype(jnp.int32)
    one_hot = (entries[:, :, None] == jnp.arange(EXPERTS, dtype=jnp.int32)[None, None, :]).astype(jnp.int32)
    earlier = (jnp.cumsum(one_hot, axis=1) - one_hot).astype(jnp.int32)
    slot_ids = jnp.sum(earlier * one_hot, axis=2).astype(jnp.int32)
    places = (jnp.arange(blocks, dtype=jnp.int32)[:, None] * CAP + slot_ids).reshape(-1).astype(jnp.int32)
    experts_flat = entries.reshape(-1)
    token_ids = (jnp.arange(TOKENS * 2, dtype=jnp.int32) // 2).astype(jnp.int32)
    padded = jnp.concatenate([tokens, jnp.zeros((1, D), tokens.dtype)], axis=0)

    def one_expert(expert):
        owners = jnp.where(experts_flat == expert, places, blocks * CAP).astype(jnp.int32)
        source_ids = jnp.full((blocks * CAP,), TOKENS, jnp.int32).at[owners].set(token_ids, mode="drop")
        expert_in = padded[source_ids]
        gate_out = jnp.dot(expert_in, gate_weight[expert], preferred_element_type=jnp.float32)
        up_out = jnp.dot(expert_in, up_weight[expert], preferred_element_type=jnp.float32)
        hidden = (jax.nn.silu(gate_out) * up_out).astype(jnp.bfloat16)
        return jnp.dot(hidden, down_weight[expert], preferred_element_type=jnp.float32).astype(jnp.bfloat16)

    expert_out = lax.map(one_expert, jnp.arange(EXPERTS, dtype=jnp.int32))
    picked = expert_out[experts_flat, places].astype(jnp.float32).reshape(TOKENS, 2, D)
    result = jnp.sum(mix_weights[:, :, None] * picked, axis=1)
    return result.astype(jnp.bfloat16)
```

```python
import functools

import jax
import jax.numpy as jnp
from jax import lax
from jax.experimental import pallas as pl
from jax.experimental.pallas import tpu as pltpu
from jax.sharding import PartitionSpec as P

MESH = pl.DeviceIdType.MESH
LANES = 128
F32 = jnp.float32
BF16 = jnp.bfloat16


def flip(index, stride):
    return index + stride - 2 * stride * lax.rem(lax.div(index, stride), 2)


def kernel(
    cfg, tok_ref, routing_ref, mix_ref, gate_ref, up_ref, down_ref, out_ref,
    w_gate, w_up, w_down, blk, st1, rl, xg, hid, terms, got1, acc, send2, got2, rl2, send3, got3,
    sem_tok, sem_gate, sem_up, sem_down,
    d1_s, d1_r, d2_s, d2_r, d3_s, d3_r, c1_s, c1_r, c2_s, c2_r, c3_s, c3_r,
):
    n_exp, n_hid, T, parts, Nc, FC, nF, NS, J, Ncol, ahead = cfg
    rows = n_hid * T
    e = lax.axis_index("expert")
    h = lax.axis_index("hidden")
    core = flip(e, 1)
    side = flip(e, 2)

    def gate_copy(i, slot):
        return pltpu.make_async_copy(
            gate_ref.at[0, :, pl.ds(pl.multiple_of(i * FC, FC), FC)], w_gate.at[slot], sem_gate.at[slot])

    def up_copy(i, slot):
        return pltpu.make_async_copy(
            up_ref.at[0, :, pl.ds(pl.multiple_of(i * FC, FC), FC)], w_up.at[slot], sem_up.at[slot])

    def down_copy(j):
        return pltpu.make_async_copy(
            down_ref.at[0, :, pl.ds(pl.multiple_of(j * Ncol, Ncol), Ncol)], w_down.at[j], sem_down.at[j])

    def tok_copy(c):
        return pltpu.make_async_copy(
            tok_ref.at[:, pl.ds(c * Nc, Nc)], blk.at[c, :, pl.ds(0, Nc)], sem_tok.at[c])

    for c in range(parts):
        tok_copy(c).start()
    for i in range(NS):
        gate_copy(i, i).start()
        up_copy(i, i).start()
    for j in range(ahead):
        down_copy(j).start()

    barrier = pltpu.get_barrier_semaphore()

    def greet(k, carry):
        pl.semaphore_signal(barrier, inc=1, device_id=(e, lax.rem(h + k, n_hid)), device_id_type=MESH)
        return carry

    lax.fori_loop(1, n_hid, greet, 0)
    pl.semaphore_signal(barrier, inc=1, device_id=(core, h), device_id_type=MESH)
    pl.semaphore_signal(barrier, inc=1, device_id=(side, h), device_id_type=MESH)

    lane = lax.broadcasted_iota(jnp.int32, (T, LANES), 1)
    named = lax.rem(lane, n_exp)
    weight = jnp.zeros((T, LANES), F32)
    for k in range(2):
        weight = weight + jnp.where(named == routing_ref[:, k:k + 1], mix_ref[:, k:k + 1], 0.0)
    high = weight.astype(BF16).astype(F32)
    middle = (weight - high).astype(BF16).astype(F32)
    low = weight - high - middle
    meta = jnp.where(lane < n_exp, high,
                     jnp.where(lane < 2 * n_exp, middle, jnp.where(lane < 3 * n_exp, low, 0.0))).astype(BF16)
    for c in range(parts):
        blk[c, :, Nc:] = meta
        tok_copy(c).wait()

    pl.semaphore_wait(barrier, n_hid + 1)

    def spread(c, k):
        to = lax.rem(h + k, n_hid)
        return pltpu.make_async_remote_copy(
            src_ref=blk.at[c], dst_ref=st1.at[c, h], send_sem=d1_s.at[c, to], recv_sem=d1_r.at[c, h],
            device_id=(e, to), device_id_type=MESH)

    def spread_in(c, k):
        src = lax.rem(h + k, n_hid)
        return pltpu.make_async_remote_copy(
            src_ref=blk.at[c], dst_ref=st1.at[c, src], send_sem=d1_s.at[c, src], recv_sem=d1_r.at[c, src],
            device_id=(e, src), device_id_type=MESH)

    def to_side(c):
        return pltpu.make_async_remote_copy(
            src_ref=xg.at[c, e], dst_ref=xg.at[c, e], send_sem=d2_s.at[c], recv_sem=d2_r.at[c],
            device_id=(side, h), device_id_type=MESH)

    def from_side(c):
        return pltpu.make_async_remote_copy(
            src_ref=xg.at[c, e], dst_ref=xg.at[c, side], send_sem=d2_s.at[c], recv_sem=d2_r.at[c],
            device_id=(side, h), device_id_type=MESH)

    def to_core(c, m):
        group = side if m else e
        return pltpu.make_async_remote_copy(
            src_ref=xg.at[c, group], dst_ref=xg.at[c, group], send_sem=d3_s.at[c, m], recv_sem=d3_r.at[c, m],
            device_id=(core, h), device_id_type=MESH)

    def from_core(c, m):
        group = flip(core, 2) if m else core
        return pltpu.make_async_remote_copy(
            src_ref=xg.at[c, e], dst_ref=xg.at[c, group], send_sem=d3_s.at[c, m], recv_sem=d3_r.at[c, m],
            device_id=(core, h), device_id_type=MESH)

    for c in range(parts):
        def body(k, carry, c=c):
            spread(c, k).start()
            return carry
        lax.fori_loop(1, n_hid, body, 0)
        st1[c, h] = blk[c]
    for c in range(parts):
        def body(k, carry, c=c):
            spread_in(c, k).wait_recv()
            return carry
        lax.fori_loop(1, n_hid, body, 0)
        for k in range(n_hid):
            rl[k * T:(k + 1) * T, :] = st1[c, k].astype(F32)
        xg[c, e] = rl[...].astype(BF16)
        to_side(c).start()
        to_core(c, 0).start()
    for c in range(parts):
        from_side(c).wait_recv()
        to_core(c, 1).start()
    for c in range(parts):
        from_core(c, 0).wait_recv()
        from_core(c, 1).wait_recv()

    def ffn(i, carry):
        slot = lax.rem(i, NS)
        gate_copy(i, slot).wait()
        up_copy(i, slot).wait()
        g = jnp.zeros((n_exp * rows, FC), F32)
        u = jnp.zeros((n_exp * rows, FC), F32)
        for c in range(parts):
            x = xg[c, :, :, 0:Nc].reshape(n_exp * rows, Nc)
            g = g + jnp.dot(x, w_gate[slot, c * Nc:(c + 1) * Nc, :], preferred_element_type=F32)
            u = u + jnp.dot(x, w_up[slot, c * Nc:(c + 1) * Nc, :], preferred_element_type=F32)
        hid[i] = (g / (1.0 + jnp.exp(-g)) * u).astype(BF16)

        @pl.when(i + NS < nF)
        def _():
            gate_copy(i + NS, slot).start()
            up_copy(i + NS, slot).start()

        @pl.when(i == max(nF - NS - 1, 0))
        def _():
            for j in range(ahead, J):
                down_copy(j).start()
        return carry

    lax.fori_loop(0, nF, ffn, 0)

    meta_all = xg[0, :, :, Nc:].reshape(n_exp * rows, LANES).astype(F32)
    lanes = lax.broadcasted_iota(jnp.int32, (n_exp * rows, LANES), 1)
    scale = jnp.sum(jnp.where(lax.rem(lanes, n_exp) == e, meta_all, 0.0), axis=1, keepdims=True)

    def give_core(j, m):
        group = flip(core, 2) if m else core
        return pltpu.make_async_remote_copy(
            src_ref=terms.at[j, group], dst_ref=got1.at[j, m], send_sem=c1_s.at[j, m], recv_sem=c1_r.at[j, m],
            device_id=(core, h), device_id_type=MESH)

    def give_side(j):
        return pltpu.make_async_remote_copy(
            src_ref=send2.at[j], dst_ref=got2.at[j], send_sem=c2_s.at[j], recv_sem=c2_r.at[j],
            device_id=(side, h), device_id_type=MESH)

    def give(j, k):
        to = lax.rem(h + k, n_hid)
        return pltpu.make_async_remote_copy(
            src_ref=send3.at[j, to], dst_ref=got3.at[j, h], send_sem=c3_s.at[j, to], recv_sem=c3_r.at[j, h],
            device_id=(e, to), device_id_type=MESH)

    def take(j, k):
        src = lax.rem(h + k, n_hid)
        return pltpu.make_async_remote_copy(
            src_ref=send3.at[j, src], dst_ref=got3.at[j, src], send_sem=c3_s.at[j, src], recv_sem=c3_r.at[j, src],
            device_id=(e, src), device_id_type=MESH)

    def step(i, carry):
        @pl.when(i < J)
        def _():
            down_copy(i).wait()
            t = jnp.zeros((n_exp * rows, Ncol), F32)
            for k in range(nF):
                t = t + jnp.dot(hid[k], w_down[i, k * FC:(k + 1) * FC, :], preferred_element_type=F32)
            terms[i] = (t * scale).reshape(n_exp, rows, Ncol)
            give_core(i, 1).start()
            give_core(i, 0).start()

        @pl.when(jnp.logical_and(i >= 1, i < J + 1))
        def _():
            j = i - 1
            give_core(j, 1).wait_recv()
            send2[j] = (terms[j, side] + got1[j, 1]).astype(BF16)
            give_side(j).start()
            give_core(j, 0).wait_recv()
            acc[j] = terms[j, e] + got1[j, 0]

        @pl.when(i >= 2)
        def _():
            j = i - 2
            give_side(j).wait_recv()
            rl2[...] = acc[j] + got2[j].astype(F32)
            for k in range(n_hid):
                send3[j, k] = rl2[k * T:(k + 1) * T, :].astype(BF16)

            def body(k, c):
                give(j, k).start()
                return c
            lax.fori_loop(1, n_hid, body, 0)
            got3[j, h] = send3[j, h]
        return carry

    lax.fori_loop(0, J + 2, step, 0)

    for j in range(J):
        def body(k, carry, j=j):
            take(j, k).wait_recv()
            return carry
        lax.fori_loop(1, n_hid, body, 0)
        out_ref[:, j * Ncol:(j + 1) * Ncol] = jnp.sum(got3[j].astype(F32), axis=0).astype(BF16)

    for c in range(parts):
        def body(k, carry, c=c):
            spread(c, k).wait_send()
            return carry
        lax.fori_loop(1, n_hid, body, 0)
        to_side(c).wait_send()
        to_core(c, 0).wait_send()
        to_core(c, 1).wait_send()

    def sent(j, carry):
        give_core(j, 0).wait_send()
        give_core(j, 1).wait_send()
        give_side(j).wait_send()

        def body(k, c):
            give(j, k).wait_send()
            return c
        return lax.fori_loop(1, n_hid, body, carry)
    lax.fori_loop(0, J, sent, 0)


def shards(tokens, routing, mix_weights, gate_weight, up_weight, down_weight):
    T, D = tokens.shape
    FFl = gate_weight.shape[2]
    n_exp = lax.axis_size("expert")
    n_hid = lax.axis_size("hidden")
    assert n_exp == 4
    parts = 2
    Nc = D // parts
    FC = min(256, FFl)
    nF = FFl // FC
    NS = min(5, nF)
    J = 8
    Ncol = D // J
    ahead = min(3, J)
    rows = n_hid * T
    Nw = Nc + LANES
    cfg = (n_exp, n_hid, T, parts, Nc, FC, nF, NS, J, Ncol, ahead)
    dma = pltpu.SemaphoreType.DMA
    scratch = [
        pltpu.VMEM((NS, D, FC), BF16),
        pltpu.VMEM((NS, D, FC), BF16),
        pltpu.VMEM((J, FFl, Ncol), BF16),
        pltpu.VMEM((parts, T, Nw), BF16),
        pltpu.VMEM((parts, n_hid, T, Nw), BF16),
        pltpu.VMEM((rows, Nw), F32),
        pltpu.VMEM((parts, n_exp, rows, Nw), BF16),
        pltpu.VMEM((nF, n_exp * rows, FC), BF16),
        pltpu.VMEM((J, n_exp, rows, Ncol), F32),
        pltpu.VMEM((J, 2, rows, Ncol), F32),
        pltpu.VMEM((J, rows, Ncol), F32),
        pltpu.VMEM((J, rows, Ncol), BF16),
        pltpu.VMEM((J, rows, Ncol), BF16),
        pltpu.VMEM((rows, Ncol), F32),
        pltpu.VMEM((J, n_hid, T, Ncol), BF16),
        pltpu.VMEM((J, n_hid, T, Ncol), BF16),
        dma((parts,)), dma((NS,)), dma((NS,)), dma((J,)),
        dma((parts, n_hid)), dma((parts, n_hid)),
        dma((parts,)), dma((parts,)),
        dma((parts, 2)), dma((parts, 2)),
        dma((J, 2)), dma((J, 2)),
        dma((J,)), dma((J,)),
        dma((J, n_hid)), dma((J, n_hid)),
    ]
    any_spec = pl.BlockSpec(memory_space=pl.ANY)
    vmem = pl.BlockSpec(memory_space=pltpu.VMEM)
    flops = 6 * n_exp * rows * D * FFl
    return pl.pallas_call(
        functools.partial(kernel, cfg),
        out_shape=jax.ShapeDtypeStruct((T, D), BF16),
        in_specs=[any_spec, vmem, vmem, any_spec, any_spec, any_spec],
        out_specs=vmem,
        scratch_shapes=scratch,
        cost_estimate=pl.CostEstimate(flops=flops, bytes_accessed=6 * D * FFl, transcendentals=0),
        compiler_params=pltpu.CompilerParams(
            collective_id=0, has_side_effects=True, vmem_limit_bytes=63 * 1024 * 1024),
    )(tokens, routing, mix_weights, gate_weight, up_weight, down_weight)


def solution(mesh):
    in_specs = (
        P(("expert", "hidden"), None),
        P(("expert", "hidden"), None),
        P(("expert", "hidden"), None),
        P("expert", None, "hidden"),
        P("expert", None, "hidden"),
        P("expert", "hidden", None),
    )
    out_specs = P(("expert", "hidden"), None)
    return jax.shard_map(shards, mesh=mesh, in_specs=in_specs, out_specs=out_specs, check_vma=False)
```

```python
import functools

import jax
import jax.numpy as jnp
from jax import lax
from jax.experimental import pallas as pl
from jax.experimental.pallas import tpu as pltpu
from jax.sharding import PartitionSpec as P

MESH = pl.DeviceIdType.MESH
LANES = 128
F32 = jnp.float32
BF16 = jnp.bfloat16


def flip(index, stride):
    return index + stride - 2 * stride * lax.rem(lax.div(index, stride), 2)


def kernel(
    cfg, tok_ref, routing_ref, mix_ref, gate_ref, up_ref, down_ref, out_ref,
    w_gu, w_down, blk, st1, rl, xg, xs, part_sum, hid, terms, got1, acc, send2, got2, rl2, send3, got3,
    sem_tok, sem_gate, sem_up, sem_down,
    d1_s, d1_r, d2_s, d2_r, d3_s, d3_r, c1_s, c1_r, c2_s, c2_r, c3_s, c3_r,
):
    n_exp, n_hid, T, parts, Nc, FC, nF, NS, J, Ncol, ahead = cfg
    rows = n_hid * T
    e = lax.axis_index("expert")
    h = lax.axis_index("hidden")
    core = flip(e, 1)
    side = flip(e, 2)

    def gate_copy(i, slot):
        return pltpu.make_async_copy(
            gate_ref.at[0, :, pl.ds(pl.multiple_of(i * FC, FC), FC)], w_gu.at[slot, :, pl.ds(0, FC)], sem_gate.at[slot])

    def up_copy(i, slot):
        return pltpu.make_async_copy(
            up_ref.at[0, :, pl.ds(pl.multiple_of(i * FC, FC), FC)], w_gu.at[slot, :, pl.ds(FC, FC)], sem_up.at[slot])

    def down_copy(j):
        return pltpu.make_async_copy(
            down_ref.at[0, :, pl.ds(pl.multiple_of(j * Ncol, Ncol), Ncol)], w_down.at[j], sem_down.at[j])

    def tok_copy(c):
        return pltpu.make_async_copy(
            tok_ref.at[:, pl.ds(c * Nc, Nc)], blk.at[c, :, pl.ds(0, Nc)], sem_tok.at[c])

    for c in range(parts):
        tok_copy(c).start()
    for i in range(NS):
        gate_copy(i, i).start()
        up_copy(i, i).start()
    for j in range(ahead):
        down_copy(j).start()

    barrier = pltpu.get_barrier_semaphore()

    def greet(k, carry):
        pl.semaphore_signal(barrier, inc=1, device_id=(e, lax.rem(h + k, n_hid)), device_id_type=MESH)
        return carry

    lax.fori_loop(1, n_hid, greet, 0)
    pl.semaphore_signal(barrier, inc=1, device_id=(core, h), device_id_type=MESH)
    pl.semaphore_signal(barrier, inc=1, device_id=(side, h), device_id_type=MESH)

    lane = lax.broadcasted_iota(jnp.int32, (T, LANES), 1)
    named = lax.rem(lane, n_exp)
    weight = jnp.zeros((T, LANES), F32)
    for k in range(2):
        weight = weight + jnp.where(named == routing_ref[:, k:k + 1], mix_ref[:, k:k + 1], 0.0)
    high = weight.astype(BF16).astype(F32)
    middle = (weight - high).astype(BF16).astype(F32)
    low = weight - high - middle
    meta = jnp.where(lane < n_exp, high,
                     jnp.where(lane < 2 * n_exp, middle, jnp.where(lane < 3 * n_exp, low, 0.0))).astype(BF16)
    for c in range(parts):
        blk[c, :, Nc:] = meta
        tok_copy(c).wait()

    pl.semaphore_wait(barrier, n_hid + 1)

    def spread(c, k):
        to = lax.rem(h + k, n_hid)
        return pltpu.make_async_remote_copy(
            src_ref=blk.at[c], dst_ref=st1.at[c, h], send_sem=d1_s.at[c], recv_sem=d1_r.at[c],
            device_id=(e, to), device_id_type=MESH)

    def peers(ref, sem):
        whole = ref.at[pl.ds(0, n_hid - 1)]
        return pltpu.make_async_copy(whole, whole, sem)

    def to_side(c):
        return pltpu.make_async_remote_copy(
            src_ref=xg.at[c, e], dst_ref=xg.at[c, e], send_sem=d2_s.at[c], recv_sem=d2_r.at[c],
            device_id=(side, h), device_id_type=MESH)

    def from_side(c):
        return pltpu.make_async_remote_copy(
            src_ref=xg.at[c, e], dst_ref=xg.at[c, side], send_sem=d2_s.at[c], recv_sem=d2_r.at[c],
            device_id=(side, h), device_id_type=MESH)

    def to_core(c, m):
        group = side if m else e
        return pltpu.make_async_remote_copy(
            src_ref=xg.at[c, group], dst_ref=xg.at[c, group], send_sem=d3_s.at[c, m], recv_sem=d3_r.at[c, m],
            device_id=(core, h), device_id_type=MESH)

    def from_core(c, m):
        group = flip(core, 2) if m else core
        return pltpu.make_async_remote_copy(
            src_ref=xg.at[c, e], dst_ref=xg.at[c, group], send_sem=d3_s.at[c, m], recv_sem=d3_r.at[c, m],
            device_id=(core, h), device_id_type=MESH)

    for c in range(parts):
        def body(k, carry, c=c):
            spread(c, k).start()
            return carry
        lax.fori_loop(1, n_hid, body, 0)
        st1[c, h] = blk[c]
    for c in range(parts):
        peers(st1.at[c], d1_r.at[c]).wait()
        for k in range(n_hid):
            rl[k * T:(k + 1) * T, :] = st1[c, k].astype(F32)
        xg[c, e] = rl[...].astype(BF16)
        to_side(c).start()
        to_core(c, 0).start()

    def forward(c):
        from_side(c).wait_recv()
        to_core(c, 1).start()

    def collect(c):
        from_core(c, 0).wait_recv()
        from_core(c, 1).wait_recv()
        xs[:, c * Nc:(c + 1) * Nc] = xg[c, :, :, 0:Nc].reshape(n_exp * rows, Nc)

    def finish(i, slot, both):
        g = both[:, 0:FC]
        hid[:, pl.ds(pl.multiple_of(i * FC, FC), FC)] = (g / (1.0 + jnp.exp(-g)) * both[:, FC:]).astype(BF16)

        @pl.when(i + NS < nF)
        def _():
            gate_copy(i + NS, slot).start()
            up_copy(i + NS, slot).start()

        @pl.when(i == max(nF - NS - 1, 0))
        def _():
            for j in range(ahead, J):
                down_copy(j).start()

    def early(c):
        def body(i, carry):
            if c == 0:
                gate_copy(i, i).wait()
                up_copy(i, i).wait()
            both = jnp.dot(xs[:, c * Nc:(c + 1) * Nc], w_gu[i, c * Nc:(c + 1) * Nc, :], preferred_element_type=F32)
            if c > 0:
                both = both + part_sum[i]
            if c < parts - 1:
                part_sum[i] = both
            else:
                finish(i, i, both)
            return carry
        return body

    cut = min(2, NS)
    forward(0)
    collect(0)
    for c in range(parts):
        lax.fori_loop(0, cut, early(c), 0)
        if c < parts - 1:
            forward(c + 1)
        lax.fori_loop(cut, NS, early(c), 0)
        if c < parts - 1:
            collect(c + 1)

    def ffn(i, carry):
        slot = lax.rem(i, NS)
        gate_copy(i, slot).wait()
        up_copy(i, slot).wait()
        finish(i, slot, jnp.dot(xs[...], w_gu[slot], preferred_element_type=F32))
        return carry

    lax.fori_loop(NS, nF, ffn, 0)

    meta_all = xg[0, :, :, Nc:].reshape(n_exp * rows, LANES).astype(F32)
    lanes = lax.broadcasted_iota(jnp.int32, (n_exp * rows, LANES), 1)
    scale = jnp.sum(jnp.where(lax.rem(lanes, n_exp) == e, meta_all, 0.0), axis=1, keepdims=True)

    def give_core(j, m):
        group = flip(core, 2) if m else core
        return pltpu.make_async_remote_copy(
            src_ref=terms.at[j, group], dst_ref=got1.at[j, m], send_sem=c1_s.at[j, m], recv_sem=c1_r.at[j, m],
            device_id=(core, h), device_id_type=MESH)

    def give_side(j):
        return pltpu.make_async_remote_copy(
            src_ref=send2.at[j], dst_ref=got2.at[j], send_sem=c2_s.at[j], recv_sem=c2_r.at[j],
            device_id=(side, h), device_id_type=MESH)

    def give(j, k):
        to = lax.rem(h + k, n_hid)
        return pltpu.make_async_remote_copy(
            src_ref=send3.at[j, to], dst_ref=got3.at[j, h], send_sem=c3_s.at[j], recv_sem=c3_r.at[j],
            device_id=(e, to), device_id_type=MESH)

    def step(i, carry):
        @pl.when(i < J)
        def _():
            down_copy(i).wait()
            t = jnp.dot(hid[...], w_down[i], preferred_element_type=F32)
            terms[i] = (t * scale).reshape(n_exp, rows, Ncol)
            give_core(i, 1).start()
            give_core(i, 0).start()

        @pl.when(jnp.logical_and(i >= 1, i < J + 1))
        def _():
            j = i - 1
            give_core(j, 1).wait_recv()
            send2[j] = (terms[j, side] + got1[j, 1]).astype(BF16)
            give_side(j).start()
            give_core(j, 0).wait_recv()
            acc[j] = terms[j, e] + got1[j, 0]

        @pl.when(i >= 2)
        def _():
            j = i - 2
            give_side(j).wait_recv()
            rl2[...] = acc[j] + got2[j].astype(F32)
            for k in range(n_hid):
                send3[j, k] = rl2[k * T:(k + 1) * T, :].astype(BF16)

            def body(k, c):
                give(j, k).start()
                return c
            lax.fori_loop(1, n_hid, body, 0)
            got3[j, h] = send3[j, h]
        return carry

    lax.fori_loop(0, J + 2, step, 0)

    for j in range(J):
        peers(got3.at[j], c3_r.at[j]).wait()
        out_ref[:, j * Ncol:(j + 1) * Ncol] = jnp.sum(got3[j].astype(F32), axis=0).astype(BF16)

    for c in range(parts):
        peers(st1.at[c], d1_s.at[c]).wait()
        to_side(c).wait_send()
        to_core(c, 0).wait_send()
        to_core(c, 1).wait_send()

    def sent(j, carry):
        give_core(j, 0).wait_send()
        give_core(j, 1).wait_send()
        give_side(j).wait_send()
        peers(send3.at[j], c3_s.at[j]).wait()
        return carry
    lax.fori_loop(0, J, sent, 0)


def shards(tokens, routing, mix_weights, gate_weight, up_weight, down_weight):
    T, D = tokens.shape
    FFl = gate_weight.shape[2]
    n_exp = lax.axis_size("expert")
    n_hid = lax.axis_size("hidden")
    assert n_exp == 4
    parts = 2
    Nc = D // parts
    FC = min(256, FFl)
    nF = FFl // FC
    NS = min(5, nF)
    J = 6
    Ncol = D // J
    ahead = min(2, J)
    rows = n_hid * T
    Nw = Nc + LANES
    cfg = (n_exp, n_hid, T, parts, Nc, FC, nF, NS, J, Ncol, ahead)
    dma = pltpu.SemaphoreType.DMA
    scratch = [
        pltpu.VMEM((NS, D, 2 * FC), BF16),
        pltpu.VMEM((J, FFl, Ncol), BF16),
        pltpu.VMEM((parts, T, Nw), BF16),
        pltpu.VMEM((parts, n_hid, T, Nw), BF16),
        pltpu.VMEM((rows, Nw), F32),
        pltpu.VMEM((parts, n_exp, rows, Nw), BF16),
        pltpu.VMEM((n_exp * rows, D), BF16),
        pltpu.VMEM((NS, n_exp * rows, 2 * FC), F32),
        pltpu.VMEM((n_exp * rows, FFl), BF16),
        pltpu.VMEM((J, n_exp, rows, Ncol), F32),
        pltpu.VMEM((J, 2, rows, Ncol), F32),
        pltpu.VMEM((J, rows, Ncol), F32),
        pltpu.VMEM((J, rows, Ncol), BF16),
        pltpu.VMEM((J, rows, Ncol), BF16),
        pltpu.VMEM((rows, Ncol), F32),
        pltpu.VMEM((J, n_hid, T, Ncol), BF16),
        pltpu.VMEM((J, n_hid, T, Ncol), BF16),
        dma((parts,)), dma((NS,)), dma((NS,)), dma((J,)),
        dma((parts,)), dma((parts,)),
        dma((parts,)), dma((parts,)),
        dma((parts, 2)), dma((parts, 2)),
        dma((J, 2)), dma((J, 2)),
        dma((J,)), dma((J,)),
        dma((J,)), dma((J,)),
    ]
    any_spec = pl.BlockSpec(memory_space=pl.ANY)
    vmem = pl.BlockSpec(memory_space=pltpu.VMEM)
    flops = 6 * n_exp * rows * D * FFl
    return pl.pallas_call(
        functools.partial(kernel, cfg),
        out_shape=jax.ShapeDtypeStruct((T, D), BF16),
        in_specs=[any_spec, vmem, vmem, any_spec, any_spec, any_spec],
        out_specs=vmem,
        scratch_shapes=scratch,
        cost_estimate=pl.CostEstimate(flops=flops, bytes_accessed=6 * D * FFl, transcendentals=0),
        compiler_params=pltpu.CompilerParams(
            collective_id=0, has_side_effects=True, vmem_limit_bytes=63 * 1024 * 1024),
    )(tokens, routing, mix_weights, gate_weight, up_weight, down_weight)


def solution(mesh):
    in_specs = (
        P(("expert", "hidden"), None),
        P(("expert", "hidden"), None),
        P(("expert", "hidden"), None),
        P("expert", None, "hidden"),
        P("expert", None, "hidden"),
        P("expert", "hidden", None),
    )
    out_specs = P(("expert", "hidden"), None)
    return jax.shard_map(shards, mesh=mesh, in_specs=in_specs, out_specs=out_specs, check_vma=False)
```

```python
import functools

import jax
import jax.numpy as jnp
from jax import lax
from jax.experimental import pallas as pl
from jax.experimental.pallas import tpu as pltpu
from jax.sharding import PartitionSpec as P

MESH = pl.DeviceIdType.MESH
LANES = 128
F32 = jnp.float32
BF16 = jnp.bfloat16


def flip(index, stride):
    return index + stride - 2 * stride * lax.rem(lax.div(index, stride), 2)


def kernel(
    cfg, tok_ref, routing_ref, mix_ref, gate_ref, up_ref, down_ref, out_ref,
    w_gate, w_up, w_down, blk, st1, rl, xg, xs, acc_g, acc_u, hid, terms, got1, acc, send2, got2, rl2, send3, got3,
    sem_tok, sem_gate, sem_up, sem_down,
    d1_s, d1_r, d2_s, d2_r, d3_s, d3_r, c1_s, c1_r, c2_s, c2_r, c3_s, c3_r,
):
    n_exp, n_hid, T, parts, Nc, KC, nK, NB, NS, first, J, Ncol = cfg
    rows = n_hid * T
    per = nK // parts
    e = lax.axis_index("expert")
    h = lax.axis_index("hidden")
    core = flip(e, 1)
    side = flip(e, 2)

    def gate_copy(i, slot):
        return pltpu.make_async_copy(
            gate_ref.at[0, pl.ds(pl.multiple_of(i * KC, KC), KC)], w_gate.at[slot], sem_gate.at[slot])

    def up_copy(i, slot):
        return pltpu.make_async_copy(
            up_ref.at[0, pl.ds(pl.multiple_of(i * KC, KC), KC)], w_up.at[slot], sem_up.at[slot])

    def down_copy(j):
        return pltpu.make_async_copy(
            down_ref.at[0, :, pl.ds(pl.multiple_of(j * Ncol, Ncol), Ncol)], w_down.at[j], sem_down.at[j])

    def tok_copy(c):
        return pltpu.make_async_copy(
            tok_ref.at[:, pl.ds(c * Nc, Nc)], blk.at[c, :, pl.ds(0, Nc)], sem_tok.at[c])

    for c in range(parts):
        tok_copy(c).start()

    queue = [("pair", i) for i in range(NS)] + [("down", j) for j in range(J)]

    def fetch(count):
        for kind, i in queue[:count]:
            if kind == "pair":
                gate_copy(i, i).start()
                up_copy(i, i).start()
            else:
                down_copy(i).start()
        del queue[:count]

    fetch(first)

    barrier = pltpu.get_barrier_semaphore()

    def greet(k, carry):
        pl.semaphore_signal(barrier, inc=1, device_id=(e, lax.rem(h + k, n_hid)), device_id_type=MESH)
        return carry

    lax.fori_loop(1, n_hid, greet, 0)
    pl.semaphore_signal(barrier, inc=1, device_id=(core, h), device_id_type=MESH)
    pl.semaphore_signal(barrier, inc=1, device_id=(side, h), device_id_type=MESH)

    lane = lax.broadcasted_iota(jnp.int32, (T, LANES), 1)
    named = lax.rem(lane, n_exp)
    weight = jnp.zeros((T, LANES), F32)
    for k in range(2):
        weight = weight + jnp.where(named == routing_ref[:, k:k + 1], mix_ref[:, k:k + 1], 0.0)
    high = weight.astype(BF16).astype(F32)
    middle = (weight - high).astype(BF16).astype(F32)
    low = weight - high - middle
    meta = jnp.where(lane < n_exp, high,
                     jnp.where(lane < 2 * n_exp, middle, jnp.where(lane < 3 * n_exp, low, 0.0))).astype(BF16)
    for c in range(parts):
        blk[c, :, Nc:] = meta
        tok_copy(c).wait()

    pl.semaphore_wait(barrier, n_hid + 1)

    def spread(c, k):
        to = lax.rem(h + k, n_hid)
        return pltpu.make_async_remote_copy(
            src_ref=blk.at[c], dst_ref=st1.at[c, h], send_sem=d1_s.at[c], recv_sem=d1_r.at[c],
            device_id=(e, to), device_id_type=MESH)

    def peers(ref, sem):
        whole = ref.at[pl.ds(0, n_hid - 1)]
        return pltpu.make_async_copy(whole, whole, sem)

    def to_side(c):
        return pltpu.make_async_remote_copy(
            src_ref=xg.at[c, e], dst_ref=xg.at[c, e], send_sem=d2_s.at[c], recv_sem=d2_r.at[c],
            device_id=(side, h), device_id_type=MESH)

    def from_side(c):
        return pltpu.make_async_remote_copy(
            src_ref=xg.at[c, e], dst_ref=xg.at[c, side], send_sem=d2_s.at[c], recv_sem=d2_r.at[c],
            device_id=(side, h), device_id_type=MESH)

    def to_core(c, m):
        group = side if m else e
        return pltpu.make_async_remote_copy(
            src_ref=xg.at[c, group], dst_ref=xg.at[c, group], send_sem=d3_s.at[c, m], recv_sem=d3_r.at[c, m],
            device_id=(core, h), device_id_type=MESH)

    def from_core(c, m):
        group = flip(core, 2) if m else core
        return pltpu.make_async_remote_copy(
            src_ref=xg.at[c, e], dst_ref=xg.at[c, group], send_sem=d3_s.at[c, m], recv_sem=d3_r.at[c, m],
            device_id=(core, h), device_id_type=MESH)

    for c in range(parts):
        def body(k, carry, c=c):
            spread(c, k).start()
            return carry
        lax.fori_loop(1, n_hid, body, 0)
        st1[c, h] = blk[c]
    fetch(2)
    for c in range(parts):
        peers(st1.at[c], d1_r.at[c]).wait()
        for k in range(n_hid):
            rl[k * T:(k + 1) * T, :] = st1[c, k].astype(F32)
        xg[c, e] = rl[...].astype(BF16)
        to_side(c).start()
        to_core(c, 0).start()
        fetch(1)

    def forward(c):
        from_side(c).wait_recv()
        to_core(c, 1).start()

    def collect(c):
        from_core(c, 0).wait_recv()
        from_core(c, 1).wait_recv()
        for q in range(per):
            xs[c * per + q] = xg[c, :, :, q * KC:(q + 1) * KC].reshape(n_exp * rows, KC)

    acc_g[...] = jnp.zeros_like(acc_g)
    acc_u[...] = jnp.zeros_like(acc_u)

    def ffn(i, carry):
        slot = lax.rem(i, NS)
        gate_copy(i, slot).wait()
        up_copy(i, slot).wait()
        x = xs[i]
        for n in range(0, acc_g.shape[1], NB):
            acc_g[:, n:n + NB] += jnp.dot(x, w_gate[slot, :, n:n + NB], preferred_element_type=F32)
            acc_u[:, n:n + NB] += jnp.dot(x, w_up[slot, :, n:n + NB], preferred_element_type=F32)

        @pl.when(i + NS < nK)
        def _():
            gate_copy(i + NS, slot).start()
            up_copy(i + NS, slot).start()

        @pl.when(i == max(nK - NS - 1, 0))
        def _():
            for j in left:
                down_copy(j).start()
        return carry

    for c in range(parts - 1):
        forward(c)
        fetch(1)
    fetch(max(0, len(queue) - J))
    left = [j for _, j in queue]
    collect(0)
    half = per // 2
    lax.fori_loop(0, half, ffn, 0)
    forward(parts - 1)
    for c in range(parts):
        if c > 0:
            collect(c)
        lo = half if c == 0 else c * per
        lax.fori_loop(lo, (c + 1) * per, ffn, 0)
    for n in range(0, acc_g.shape[1], NB):
        g = acc_g[:, n:n + NB]
        hid[:, n:n + NB] = (g / (1.0 + jnp.exp(-g)) * acc_u[:, n:n + NB]).astype(BF16)

    meta_all = xg[0, :, :, Nc:].reshape(n_exp * rows, LANES).astype(F32)
    lanes = lax.broadcasted_iota(jnp.int32, (n_exp * rows, LANES), 1)
    scale = jnp.sum(jnp.where(lax.rem(lanes, n_exp) == e, meta_all, 0.0), axis=1, keepdims=True)

    def give_core(j, m):
        group = flip(core, 2) if m else core
        return pltpu.make_async_remote_copy(
            src_ref=terms.at[j, group], dst_ref=got1.at[j, m], send_sem=c1_s.at[j, m], recv_sem=c1_r.at[j, m],
            device_id=(core, h), device_id_type=MESH)

    def give_side(j):
        return pltpu.make_async_remote_copy(
            src_ref=send2.at[j], dst_ref=got2.at[j], send_sem=c2_s.at[j], recv_sem=c2_r.at[j],
            device_id=(side, h), device_id_type=MESH)

    def give(j, k):
        to = lax.rem(h + k, n_hid)
        return pltpu.make_async_remote_copy(
            src_ref=send3.at[j, to], dst_ref=got3.at[j, h], send_sem=c3_s.at[j], recv_sem=c3_r.at[j],
            device_id=(e, to), device_id_type=MESH)

    def step(i, carry):
        @pl.when(i < J)
        def _():
            down_copy(i).wait()
            t = jnp.dot(hid[...], w_down[i], preferred_element_type=F32)
            terms[i] = (t * scale).reshape(n_exp, rows, Ncol)
            give_core(i, 1).start()
            give_core(i, 0).start()

        @pl.when(jnp.logical_and(i >= 1, i < J + 1))
        def _():
            j = i - 1
            give_core(j, 1).wait_recv()
            send2[j] = (terms[j, side] + got1[j, 1]).astype(BF16)
            give_side(j).start()
            give_core(j, 0).wait_recv()
            acc[j] = terms[j, e] + got1[j, 0]

        @pl.when(i >= 2)
        def _():
            j = i - 2
            give_side(j).wait_recv()
            rl2[...] = acc[j] + got2[j].astype(F32)
            for k in range(n_hid):
                send3[j, k] = rl2[k * T:(k + 1) * T, :].astype(BF16)

            def body(k, c):
                give(j, k).start()
                return c
            lax.fori_loop(1, n_hid, body, 0)
            got3[j, h] = send3[j, h]
        return carry

    lax.fori_loop(0, J + 2, step, 0)

    for j in range(J):
        peers(got3.at[j], c3_r.at[j]).wait()
        out_ref[:, j * Ncol:(j + 1) * Ncol] = jnp.sum(got3[j].astype(F32), axis=0).astype(BF16)

    for c in range(parts):
        peers(st1.at[c], d1_s.at[c]).wait()
        to_side(c).wait_send()
        to_core(c, 0).wait_send()
        to_core(c, 1).wait_send()

    def sent(j, carry):
        give_core(j, 0).wait_send()
        give_core(j, 1).wait_send()
        give_side(j).wait_send()
        peers(send3.at[j], c3_s.at[j]).wait()
        return carry
    lax.fori_loop(0, J, sent, 0)


def shards(tokens, routing, mix_weights, gate_weight, up_weight, down_weight):
    T, D = tokens.shape
    FFl = gate_weight.shape[2]
    n_exp = lax.axis_size("expert")
    n_hid = lax.axis_size("hidden")
    assert n_exp == 4
    parts = 3
    Nc = D // parts
    KC = 512
    nK = D // KC
    NB = min(512, FFl)
    NS = min(7, nK)
    first = 3
    J = 6
    Ncol = D // J
    rows = n_hid * T
    Nw = Nc + LANES
    cfg = (n_exp, n_hid, T, parts, Nc, KC, nK, NB, NS, first, J, Ncol)
    dma = pltpu.SemaphoreType.DMA
    scratch = [
        pltpu.VMEM((NS, KC, FFl), BF16),
        pltpu.VMEM((NS, KC, FFl), BF16),
        pltpu.VMEM((J, FFl, Ncol), BF16),
        pltpu.VMEM((parts, T, Nw), BF16),
        pltpu.VMEM((parts, n_hid, T, Nw), BF16),
        pltpu.VMEM((rows, Nw), F32),
        pltpu.VMEM((parts, n_exp, rows, Nw), BF16),
        pltpu.VMEM((nK, n_exp * rows, KC), BF16),
        pltpu.VMEM((n_exp * rows, FFl), F32),
        pltpu.VMEM((n_exp * rows, FFl), F32),
        pltpu.VMEM((n_exp * rows, FFl), BF16),
        pltpu.VMEM((J, n_exp, rows, Ncol), F32),
        pltpu.VMEM((J, 2, rows, Ncol), F32),
        pltpu.VMEM((J, rows, Ncol), F32),
        pltpu.VMEM((J, rows, Ncol), BF16),
        pltpu.VMEM((J, rows, Ncol), BF16),
        pltpu.VMEM((rows, Ncol), F32),
        pltpu.VMEM((J, n_hid, T, Ncol), BF16),
        pltpu.VMEM((J, n_hid, T, Ncol), BF16),
        dma((parts,)), dma((NS,)), dma((NS,)), dma((J,)),
        dma((parts,)), dma((parts,)),
        dma((parts,)), dma((parts,)),
        dma((parts, 2)), dma((parts, 2)),
        dma((J, 2)), dma((J, 2)),
        dma((J,)), dma((J,)),
        dma((J,)), dma((J,)),
    ]
    any_spec = pl.BlockSpec(memory_space=pl.ANY)
    vmem = pl.BlockSpec(memory_space=pltpu.VMEM)
    flops = 6 * n_exp * rows * D * FFl
    return pl.pallas_call(
        functools.partial(kernel, cfg),
        out_shape=jax.ShapeDtypeStruct((T, D), BF16),
        in_specs=[any_spec, vmem, vmem, any_spec, any_spec, any_spec],
        out_specs=vmem,
        scratch_shapes=scratch,
        cost_estimate=pl.CostEstimate(flops=flops, bytes_accessed=6 * D * FFl, transcendentals=0),
        compiler_params=pltpu.CompilerParams(
            collective_id=0, has_side_effects=True, vmem_limit_bytes=63 * 1024 * 1024),
    )(tokens, routing, mix_weights, gate_weight, up_weight, down_weight)


def solution(mesh):
    in_specs = (
        P(("expert", "hidden"), None),
        P(("expert", "hidden"), None),
        P(("expert", "hidden"), None),
        P("expert", None, "hidden"),
        P("expert", None, "hidden"),
        P("expert", "hidden", None),
    )
    out_specs = P(("expert", "hidden"), None)
    return jax.shard_map(shards, mesh=mesh, in_specs=in_specs, out_specs=out_specs, check_vma=False)
```

```python
import functools

import jax
import jax.numpy as jnp
from jax import lax
from jax.experimental import pallas as pl
from jax.experimental.pallas import tpu as pltpu
from jax.sharding import PartitionSpec as P

MESH = pl.DeviceIdType.MESH
LANES = 128
F32 = jnp.float32
BF16 = jnp.bfloat16


def flip(index, stride):
    return index + stride - 2 * stride * lax.rem(lax.div(index, stride), 2)


def kernel(
    cfg, tok_ref, routing_hbm, mix_hbm, gate_ref, up_ref, down_ref, out_ref,
    routing_ref, mix_ref, w_gate, w_up, w_down, blk, st1, rl, xg, xs, acc_g, acc_u, hid, terms, got1, acc, send2, got2, rl2, send3, got3,
    sem_tok, sem_small, sem_gate, sem_up, sem_down,
    d1_s, d1_r, d2_s, d2_r, d3_s, d3_r, c1_s, c1_r, c2_s, c2_r, c3_s, c3_r,
):
    n_exp, n_hid, T, parts, Nc, KC, nK, NB, NS, first, J, Ncol = cfg
    rows = n_hid * T
    per = nK // parts
    e = lax.axis_index("expert")
    h = lax.axis_index("hidden")
    core = flip(e, 1)
    side = flip(e, 2)

    def gate_copy(i, slot):
        return pltpu.make_async_copy(
            gate_ref.at[0, pl.ds(pl.multiple_of(i * KC, KC), KC)], w_gate.at[slot], sem_gate.at[slot])

    def up_copy(i, slot):
        return pltpu.make_async_copy(
            up_ref.at[0, pl.ds(pl.multiple_of(i * KC, KC), KC)], w_up.at[slot], sem_up.at[slot])

    def down_copy(j):
        return pltpu.make_async_copy(
            down_ref.at[0, :, pl.ds(pl.multiple_of(j * Ncol, Ncol), Ncol)], w_down.at[j], sem_down.at[j])

    def tok_copy(c):
        return pltpu.make_async_copy(
            tok_ref.at[:, pl.ds(c * Nc, Nc)], blk.at[c, :, pl.ds(0, Nc)], sem_tok.at[c])

    small = [pltpu.make_async_copy(routing_hbm, routing_ref, sem_small.at[0]),
             pltpu.make_async_copy(mix_hbm, mix_ref, sem_small.at[1])]
    for copy in small:
        copy.start()
    for c in range(parts):
        tok_copy(c).start()

    queue = [("pair", i) for i in range(NS)] + [("down", j) for j in range(J)]

    def fetch(count):
        for kind, i in queue[:count]:
            if kind == "pair":
                gate_copy(i, i).start(priority=1)
                up_copy(i, i).start(priority=1)
            else:
                down_copy(i).start(priority=1)
        del queue[:count]

    fetch(first)

    barrier = pltpu.get_barrier_semaphore()

    def greet(k, carry):
        pl.semaphore_signal(barrier, inc=1, device_id=(e, lax.rem(h + k, n_hid)), device_id_type=MESH)
        return carry

    lax.fori_loop(1, n_hid, greet, 0)
    pl.semaphore_signal(barrier, inc=1, device_id=(core, h), device_id_type=MESH)
    pl.semaphore_signal(barrier, inc=1, device_id=(side, h), device_id_type=MESH)

    for copy in small:
        copy.wait()
    lane = lax.broadcasted_iota(jnp.int32, (T, LANES), 1)
    named = lax.rem(lane, n_exp)
    weight = jnp.zeros((T, LANES), F32)
    for k in range(2):
        weight = weight + jnp.where(named == routing_ref[:, k:k + 1], mix_ref[:, k:k + 1], 0.0)
    high = weight.astype(BF16).astype(F32)
    middle = (weight - high).astype(BF16).astype(F32)
    low = weight - high - middle
    meta = jnp.where(lane < n_exp, high,
                     jnp.where(lane < 2 * n_exp, middle, jnp.where(lane < 3 * n_exp, low, 0.0))).astype(BF16)
    for c in range(parts):
        blk[c, :, Nc:] = meta
        tok_copy(c).wait()

    pl.semaphore_wait(barrier, n_hid + 1)

    def spread(c, k):
        to = lax.rem(h + k, n_hid)
        return pltpu.make_async_remote_copy(
            src_ref=blk.at[c], dst_ref=st1.at[c, h], send_sem=d1_s.at[c], recv_sem=d1_r.at[c],
            device_id=(e, to), device_id_type=MESH)

    def peers(ref, sem):
        whole = ref.at[pl.ds(0, n_hid - 1)]
        return pltpu.make_async_copy(whole, whole, sem)

    def to_side(c):
        return pltpu.make_async_remote_copy(
            src_ref=xg.at[c, e], dst_ref=xg.at[c, e], send_sem=d2_s.at[c], recv_sem=d2_r.at[c],
            device_id=(side, h), device_id_type=MESH)

    def from_side(c):
        return pltpu.make_async_remote_copy(
            src_ref=xg.at[c, e], dst_ref=xg.at[c, side], send_sem=d2_s.at[c], recv_sem=d2_r.at[c],
            device_id=(side, h), device_id_type=MESH)

    def to_core(c, m):
        group = side if m else e
        return pltpu.make_async_remote_copy(
            src_ref=xg.at[c, group], dst_ref=xg.at[c, group], send_sem=d3_s.at[c, m], recv_sem=d3_r.at[c, m],
            device_id=(core, h), device_id_type=MESH)

    def from_core(c, m):
        group = flip(core, 2) if m else core
        return pltpu.make_async_remote_copy(
            src_ref=xg.at[c, e], dst_ref=xg.at[c, group], send_sem=d3_s.at[c, m], recv_sem=d3_r.at[c, m],
            device_id=(core, h), device_id_type=MESH)

    for c in range(parts):
        def body(k, carry, c=c):
            spread(c, k).start()
            return carry
        lax.fori_loop(1, n_hid, body, 0)
        st1[c, h] = blk[c]
    fetch(2)
    for c in range(parts):
        peers(st1.at[c], d1_r.at[c]).wait()
        for k in range(n_hid):
            rl[k * T:(k + 1) * T, :] = st1[c, k].astype(F32)
        xg[c, e] = rl[...].astype(BF16)
        to_side(c).start()
        to_core(c, 0).start()
        fetch(1)

    def forward(c):
        from_side(c).wait_recv()
        to_core(c, 1).start()

    def collect(c):
        from_core(c, 0).wait_recv()
        from_core(c, 1).wait_recv()
        for q in range(per):
            xs[c * per + q] = xg[c, :, :, q * KC:(q + 1) * KC].reshape(n_exp * rows, KC)

    acc_g[...] = jnp.zeros_like(acc_g)
    acc_u[...] = jnp.zeros_like(acc_u)

    def ffn(i, carry):
        slot = lax.rem(i, NS)
        gate_copy(i, slot).wait()
        up_copy(i, slot).wait()
        x = xs[i]
        for n in range(0, acc_g.shape[1], NB):
            acc_g[:, n:n + NB] += jnp.dot(x, w_gate[slot, :, n:n + NB], preferred_element_type=F32)
            acc_u[:, n:n + NB] += jnp.dot(x, w_up[slot, :, n:n + NB], preferred_element_type=F32)

        @pl.when(i + NS < nK)
        def _():
            gate_copy(i + NS, slot).start(priority=1)
            up_copy(i + NS, slot).start(priority=1)

        @pl.when(i == max(nK - NS - 1, 0))
        def _():
            for j in left:
                down_copy(j).start(priority=1)
        return carry

    for c in range(parts - 1):
        forward(c)
        fetch(1)
    fetch(max(0, len(queue) - J))
    left = [j for _, j in queue]
    collect(0)
    half = per // 2
    lax.fori_loop(0, half, ffn, 0)
    forward(parts - 1)
    for c in range(parts):
        if c > 0:
            collect(c)
        lo = half if c == 0 else c * per
        lax.fori_loop(lo, (c + 1) * per, ffn, 0)
    for n in range(0, acc_g.shape[1], NB):
        g = acc_g[:, n:n + NB]
        hid[:, n:n + NB] = (g / (1.0 + jnp.exp(-g)) * acc_u[:, n:n + NB]).astype(BF16)

    meta_all = xg[0, :, :, Nc:].reshape(n_exp * rows, LANES).astype(F32)
    lanes = lax.broadcasted_iota(jnp.int32, (n_exp * rows, LANES), 1)
    scale = jnp.sum(jnp.where(lax.rem(lanes, n_exp) == e, meta_all, 0.0), axis=1, keepdims=True)

    def give_core(j, m):
        group = flip(core, 2) if m else core
        return pltpu.make_async_remote_copy(
            src_ref=terms.at[j, group], dst_ref=got1.at[j, m], send_sem=c1_s.at[j, m], recv_sem=c1_r.at[j, m],
            device_id=(core, h), device_id_type=MESH)

    def give_side(j):
        return pltpu.make_async_remote_copy(
            src_ref=send2.at[j], dst_ref=got2.at[j], send_sem=c2_s.at[j], recv_sem=c2_r.at[j],
            device_id=(side, h), device_id_type=MESH)

    def give(j, k):
        to = lax.rem(h + k, n_hid)
        return pltpu.make_async_remote_copy(
            src_ref=send3.at[j, to], dst_ref=got3.at[j, h], send_sem=c3_s.at[j], recv_sem=c3_r.at[j],
            device_id=(e, to), device_id_type=MESH)

    def step(i, carry):
        @pl.when(i < J)
        def _():
            down_copy(i).wait()
            t = jnp.dot(hid[...], w_down[i], preferred_element_type=F32)
            terms[i] = (t * scale).reshape(n_exp, rows, Ncol)
            give_core(i, 1).start()
            give_core(i, 0).start()

        @pl.when(jnp.logical_and(i >= 1, i < J + 1))
        def _():
            j = i - 1
            give_core(j, 1).wait_recv()
            send2[j] = (terms[j, side] + got1[j, 1]).astype(BF16)
            give_side(j).start()
            give_core(j, 0).wait_recv()
            acc[j] = terms[j, e] + got1[j, 0]

        @pl.when(i >= 2)
        def _():
            j = i - 2
            give_side(j).wait_recv()
            rl2[...] = acc[j] + got2[j].astype(F32)
            for k in range(n_hid):
                send3[j, k] = rl2[k * T:(k + 1) * T, :].astype(BF16)

            def body(k, c):
                give(j, k).start()
                return c
            lax.fori_loop(1, n_hid, body, 0)
            got3[j, h] = send3[j, h]
        return carry

    lax.fori_loop(0, J + 2, step, 0)

    for j in range(J):
        peers(got3.at[j], c3_r.at[j]).wait()
        out_ref[:, j * Ncol:(j + 1) * Ncol] = jnp.sum(got3[j].astype(F32), axis=0)

    for c in range(parts):
        peers(st1.at[c], d1_s.at[c]).wait()
        to_side(c).wait_send()
        to_core(c, 0).wait_send()
        to_core(c, 1).wait_send()

    def sent(j, carry):
        give_core(j, 0).wait_send()
        give_core(j, 1).wait_send()
        give_side(j).wait_send()
        peers(send3.at[j], c3_s.at[j]).wait()
        return carry
    lax.fori_loop(0, J, sent, 0)


def shards(tokens, routing, mix_weights, gate_weight, up_weight, down_weight):
    T, D = tokens.shape
    FFl = gate_weight.shape[2]
    n_exp = lax.axis_size("expert")
    n_hid = lax.axis_size("hidden")
    assert n_exp == 4
    parts = 3
    Nc = D // parts
    KC = 512
    nK = D // KC
    NB = min(512, FFl)
    NS = min(7, nK)
    first = 3
    J = 6
    Ncol = D // J
    rows = n_hid * T
    Nw = Nc + LANES
    cfg = (n_exp, n_hid, T, parts, Nc, KC, nK, NB, NS, first, J, Ncol)
    dma = pltpu.SemaphoreType.DMA
    scratch = [
        pltpu.VMEM(routing.shape, jnp.int32),
        pltpu.VMEM(mix_weights.shape, F32),
        pltpu.VMEM((NS, KC, FFl), BF16),
        pltpu.VMEM((NS, KC, FFl), BF16),
        pltpu.VMEM((J, FFl, Ncol), BF16),
        pltpu.VMEM((parts, T, Nw), BF16),
        pltpu.VMEM((parts, n_hid, T, Nw), BF16),
        pltpu.VMEM((rows, Nw), F32),
        pltpu.VMEM((parts, n_exp, rows, Nw), BF16),
        pltpu.VMEM((nK, n_exp * rows, KC), BF16),
        pltpu.VMEM((n_exp * rows, FFl), F32),
        pltpu.VMEM((n_exp * rows, FFl), F32),
        pltpu.VMEM((n_exp * rows, FFl), BF16),
        pltpu.VMEM((J, n_exp, rows, Ncol), F32),
        pltpu.VMEM((J, 2, rows, Ncol), F32),
        pltpu.VMEM((J, rows, Ncol), F32),
        pltpu.VMEM((J, rows, Ncol), BF16),
        pltpu.VMEM((J, rows, Ncol), BF16),
        pltpu.VMEM((rows, Ncol), F32),
        pltpu.VMEM((J, n_hid, T, Ncol), BF16),
        pltpu.VMEM((J, n_hid, T, Ncol), BF16),
        dma((parts,)), dma((2,)), dma((NS,)), dma((NS,)), dma((J,)),
        dma((parts,)), dma((parts,)),
        dma((parts,)), dma((parts,)),
        dma((parts, 2)), dma((parts, 2)),
        dma((J, 2)), dma((J, 2)),
        dma((J,)), dma((J,)),
        dma((J,)), dma((J,)),
    ]
    any_spec = pl.BlockSpec(memory_space=pl.ANY)
    vmem = pl.BlockSpec(memory_space=pltpu.VMEM)
    flops = 6 * n_exp * rows * D * FFl
    return pl.pallas_call(
        functools.partial(kernel, cfg),
        out_shape=jax.ShapeDtypeStruct((T, D), F32),
        in_specs=[any_spec] * 6,
        out_specs=vmem,
        scratch_shapes=scratch,
        cost_estimate=pl.CostEstimate(flops=flops, bytes_accessed=6 * D * FFl, transcendentals=0),
        compiler_params=pltpu.CompilerParams(
            collective_id=0, has_side_effects=True, vmem_limit_bytes=63 * 1024 * 1024),
    )(tokens, routing, mix_weights, gate_weight, up_weight, down_weight).astype(BF16)


def solution(mesh):
    in_specs = (
        P(("expert", "hidden"), None),
        P(("expert", "hidden"), None),
        P(("expert", "hidden"), None),
        P("expert", None, "hidden"),
        P("expert", None, "hidden"),
        P("expert", "hidden", None),
    )
    out_specs = P(("expert", "hidden"), None)
    return jax.shard_map(shards, mesh=mesh, in_specs=in_specs, out_specs=out_specs, check_vma=False)
```

```python
import functools

import jax
import jax.numpy as jnp
from jax import lax
from jax.experimental import pallas as pl
from jax.experimental.pallas import tpu as pltpu
from jax.sharding import PartitionSpec as P

MESH = pl.DeviceIdType.MESH
LANES = 128
F32 = jnp.float32
BF16 = jnp.bfloat16


def flip(index, stride):
    return index + stride - 2 * stride * lax.rem(lax.div(index, stride), 2)


def kernel(
    cfg, tok_ref, routing_hbm, mix_hbm, gate_ref, up_ref, down_ref, out_ref,
    routing_ref, mix_ref, w_gate, w_up, w_down, blk, st1, rl, xg, xs, acc_g, acc_u, hid, terms, got1, acc, send2, got2, rl2, send3, got3,
    sem_tok, sem_small, sem_gate, sem_up, sem_down,
    d1_s, d1_r, d2_s, d2_r, d3_s, d3_r, c1_s, c1_r, c2_s, c2_r, c3_s, c3_r,
):
    n_exp, n_hid, T, parts, Nc, KC, nK, NB, NS, first, J, Ncol = cfg
    rows = n_hid * T
    per = nK // parts
    e = lax.axis_index("expert")
    h = lax.axis_index("hidden")
    core = flip(e, 1)
    side = flip(e, 2)

    def gate_copy(i, slot):
        return pltpu.make_async_copy(
            gate_ref.at[0, pl.ds(pl.multiple_of(i * KC, KC), KC)], w_gate.at[slot], sem_gate.at[slot])

    def up_copy(i, slot):
        return pltpu.make_async_copy(
            up_ref.at[0, pl.ds(pl.multiple_of(i * KC, KC), KC)], w_up.at[slot], sem_up.at[slot])

    def down_copy(j):
        return pltpu.make_async_copy(
            down_ref.at[0, :, pl.ds(pl.multiple_of(j * Ncol, Ncol), Ncol)], w_down.at[j], sem_down.at[j])

    def tok_copy(c):
        return pltpu.make_async_copy(
            tok_ref.at[:, pl.ds(c * Nc, Nc)], blk.at[c, :, pl.ds(0, Nc)], sem_tok.at[c])

    small = [pltpu.make_async_copy(routing_hbm, routing_ref, sem_small.at[0]),
             pltpu.make_async_copy(mix_hbm, mix_ref, sem_small.at[1])]
    for copy in small:
        copy.start()
    for c in range(parts):
        tok_copy(c).start()

    queue = [("pair", i) for i in range(NS)] + [("down", j) for j in range(J)]

    def fetch(count):
        for kind, i in queue[:count]:
            if kind == "pair":
                gate_copy(i, i).start(priority=1)
                up_copy(i, i).start(priority=1)
            else:
                down_copy(i).start(priority=1)
        del queue[:count]

    fetch(first)

    barrier = pltpu.get_barrier_semaphore()

    def greet(k, carry):
        pl.semaphore_signal(barrier, inc=1, device_id=(e, lax.rem(h + k, n_hid)), device_id_type=MESH)
        return carry

    lax.fori_loop(1, n_hid, greet, 0)
    pl.semaphore_signal(barrier, inc=1, device_id=(core, h), device_id_type=MESH)
    pl.semaphore_signal(barrier, inc=1, device_id=(side, h), device_id_type=MESH)

    for copy in small:
        copy.wait()
    lane = lax.broadcasted_iota(jnp.int32, (T, LANES), 1)
    named = lax.rem(lane, n_exp)
    weight = jnp.zeros((T, LANES), F32)
    for k in range(2):
        weight = weight + jnp.where(named == routing_ref[:, k:k + 1], mix_ref[:, k:k + 1], 0.0)
    high = weight.astype(BF16).astype(F32)
    middle = (weight - high).astype(BF16).astype(F32)
    low = weight - high - middle
    meta = jnp.where(lane < n_exp, high,
                     jnp.where(lane < 2 * n_exp, middle, jnp.where(lane < 3 * n_exp, low, 0.0))).astype(BF16)
    for c in range(parts):
        blk[c, :, Nc:] = meta
        tok_copy(c).wait()

    pl.semaphore_wait(barrier, n_hid + 1)

    def spread(c, k):
        to = lax.rem(h + k, n_hid)
        return pltpu.make_async_remote_copy(
            src_ref=blk.at[c], dst_ref=st1.at[c, h], send_sem=d1_s.at[c], recv_sem=d1_r.at[c],
            device_id=(e, to), device_id_type=MESH)

    def peers(ref, sem):
        whole = ref.at[pl.ds(0, n_hid - 1)]
        return pltpu.make_async_copy(whole, whole, sem)

    def to_side(c):
        return pltpu.make_async_remote_copy(
            src_ref=xg.at[c, e], dst_ref=xg.at[c, e], send_sem=d2_s.at[c], recv_sem=d2_r.at[c],
            device_id=(side, h), device_id_type=MESH)

    def from_side(c):
        return pltpu.make_async_remote_copy(
            src_ref=xg.at[c, e], dst_ref=xg.at[c, side], send_sem=d2_s.at[c], recv_sem=d2_r.at[c],
            device_id=(side, h), device_id_type=MESH)

    def to_core(c, m):
        group = side if m else e
        return pltpu.make_async_remote_copy(
            src_ref=xg.at[c, group], dst_ref=xg.at[c, group], send_sem=d3_s.at[c, m], recv_sem=d3_r.at[c, m],
            device_id=(core, h), device_id_type=MESH)

    def from_core(c, m):
        group = flip(core, 2) if m else core
        return pltpu.make_async_remote_copy(
            src_ref=xg.at[c, e], dst_ref=xg.at[c, group], send_sem=d3_s.at[c, m], recv_sem=d3_r.at[c, m],
            device_id=(core, h), device_id_type=MESH)

    for c in range(parts):
        def body(k, carry, c=c):
            spread(c, k).start()
            return carry
        lax.fori_loop(1, n_hid, body, 0)
        st1[c, h] = blk[c]
    fetch(2)
    for c in range(parts):
        peers(st1.at[c], d1_r.at[c]).wait()
        for k in range(n_hid):
            rl[k * T:(k + 1) * T, :] = st1[c, k].astype(F32)
        xg[c, e] = rl[...].astype(BF16)
        to_side(c).start()
        to_core(c, 0).start()
        fetch(1)

    def forward(c):
        from_side(c).wait_recv()
        to_core(c, 1).start()

    def collect(c):
        from_core(c, 0).wait_recv()
        from_core(c, 1).wait_recv()
        for q in range(per):
            xs[c * per + q] = xg[c, :, :, q * KC:(q + 1) * KC].reshape(n_exp * rows, KC)

    acc_g[...] = jnp.zeros_like(acc_g)
    acc_u[...] = jnp.zeros_like(acc_u)

    def ffn(i, carry):
        slot = lax.rem(i, NS)
        gate_copy(i, slot).wait()
        up_copy(i, slot).wait()
        x = xs[i]
        for n in range(0, acc_g.shape[1], NB):
            acc_g[:, n:n + NB] += jnp.dot(x, w_gate[slot, :, n:n + NB], preferred_element_type=F32)
            acc_u[:, n:n + NB] += jnp.dot(x, w_up[slot, :, n:n + NB], preferred_element_type=F32)

        @pl.when(i + NS < nK)
        def _():
            gate_copy(i + NS, slot).start(priority=1)
            up_copy(i + NS, slot).start(priority=1)

        @pl.when(i == max(nK - NS - 1, 0))
        def _():
            for j in left:
                down_copy(j).start(priority=1)
        return carry

    for c in range(parts - 1):
        forward(c)
        fetch(1)
    fetch(max(0, len(queue) - J))
    left = [j for _, j in queue]
    collect(0)
    half = per // 2
    lax.fori_loop(0, half, ffn, 0)
    forward(parts - 1)
    for c in range(parts):
        if c > 0:
            collect(c)
        lo = half if c == 0 else c * per
        lax.fori_loop(lo, (c + 1) * per, ffn, 0)
    SB = min(512, acc_g.shape[1])
    for n in range(0, acc_g.shape[1], SB):
        g = acc_g[:, n:n + SB]
        hid[:, n:n + SB] = (g / (1.0 + jnp.exp(-g)) * acc_u[:, n:n + SB]).astype(BF16)

    meta_all = xg[0, :, :, Nc:].reshape(n_exp * rows, LANES).astype(F32)
    lanes = lax.broadcasted_iota(jnp.int32, (n_exp * rows, LANES), 1)
    scale = jnp.sum(jnp.where(lax.rem(lanes, n_exp) == e, meta_all, 0.0), axis=1, keepdims=True)

    def give_core(j, m):
        group = flip(core, 2) if m else core
        return pltpu.make_async_remote_copy(
            src_ref=terms.at[j, group], dst_ref=got1.at[j, m], send_sem=c1_s.at[j, m], recv_sem=c1_r.at[j, m],
            device_id=(core, h), device_id_type=MESH)

    def give_side(j):
        return pltpu.make_async_remote_copy(
            src_ref=send2.at[j], dst_ref=got2.at[j], send_sem=c2_s.at[j], recv_sem=c2_r.at[j],
            device_id=(side, h), device_id_type=MESH)

    def give(j, k):
        to = lax.rem(h + k, n_hid)
        return pltpu.make_async_remote_copy(
            src_ref=send3.at[j, to], dst_ref=got3.at[j, h], send_sem=c3_s.at[j], recv_sem=c3_r.at[j],
            device_id=(e, to), device_id_type=MESH)

    def step(i, carry):
        @pl.when(i < J)
        def _():
            down_copy(i).wait()
            t = jnp.dot(hid[...], w_down[i], preferred_element_type=F32)
            terms[i] = (t * scale).reshape(n_exp, rows, Ncol)
            give_core(i, 1).start()
            give_core(i, 0).start()

        @pl.when(jnp.logical_and(i >= 1, i < J + 1))
        def _():
            j = i - 1
            give_core(j, 1).wait_recv()
            send2[j] = (terms[j, side] + got1[j, 1]).astype(BF16)
            give_side(j).start()
            give_core(j, 0).wait_recv()
            acc[j] = terms[j, e] + got1[j, 0]

        @pl.when(i >= 2)
        def _():
            j = i - 2
            give_side(j).wait_recv()
            rl2[...] = acc[j] + got2[j].astype(F32)
            for k in range(n_hid):
                send3[j, k] = rl2[k * T:(k + 1) * T, :].astype(BF16)

            def body(k, c):
                give(j, k).start()
                return c
            lax.fori_loop(1, n_hid, body, 0)
            got3[j, h] = send3[j, h]
        return carry

    lax.fori_loop(0, J + 2, step, 0)

    for j in range(J):
        peers(got3.at[j], c3_r.at[j]).wait()
        out_ref[:, j * Ncol:(j + 1) * Ncol] = jnp.sum(got3[j].astype(F32), axis=0)

    for c in range(parts):
        peers(st1.at[c], d1_s.at[c]).wait()
        to_side(c).wait_send()
        to_core(c, 0).wait_send()
        to_core(c, 1).wait_send()

    def sent(j, carry):
        give_core(j, 0).wait_send()
        give_core(j, 1).wait_send()
        give_side(j).wait_send()
        peers(send3.at[j], c3_s.at[j]).wait()
        return carry
    lax.fori_loop(0, J, sent, 0)


def shards(tokens, routing, mix_weights, gate_weight, up_weight, down_weight):
    T, D = tokens.shape
    FFl = gate_weight.shape[2]
    n_exp = lax.axis_size("expert")
    n_hid = lax.axis_size("hidden")
    assert n_exp == 4
    parts = 3
    Nc = D // parts
    KC = 512
    nK = D // KC
    NB = min(1024, FFl)
    NS = min(7, nK)
    first = 3
    J = 6
    Ncol = D // J
    rows = n_hid * T
    Nw = Nc + LANES
    cfg = (n_exp, n_hid, T, parts, Nc, KC, nK, NB, NS, first, J, Ncol)
    dma = pltpu.SemaphoreType.DMA
    scratch = [
        pltpu.VMEM(routing.shape, jnp.int32),
        pltpu.VMEM(mix_weights.shape, F32),
        pltpu.VMEM((NS, KC, FFl), BF16),
        pltpu.VMEM((NS, KC, FFl), BF16),
        pltpu.VMEM((J, FFl, Ncol), BF16),
        pltpu.VMEM((parts, T, Nw), BF16),
        pltpu.VMEM((parts, n_hid, T, Nw), BF16),
        pltpu.VMEM((rows, Nw), F32),
        pltpu.VMEM((parts, n_exp, rows, Nw), BF16),
        pltpu.VMEM((nK, n_exp * rows, KC), BF16),
        pltpu.VMEM((n_exp * rows, FFl), F32),
        pltpu.VMEM((n_exp * rows, FFl), F32),
        pltpu.VMEM((n_exp * rows, FFl), BF16),
        pltpu.VMEM((J, n_exp, rows, Ncol), F32),
        pltpu.VMEM((J, 2, rows, Ncol), F32),
        pltpu.VMEM((J, rows, Ncol), F32),
        pltpu.VMEM((J, rows, Ncol), BF16),
        pltpu.VMEM((J, rows, Ncol), BF16),
        pltpu.VMEM((rows, Ncol), F32),
        pltpu.VMEM((J, n_hid, T, Ncol), BF16),
        pltpu.VMEM((J, n_hid, T, Ncol), BF16),
        dma((parts,)), dma((2,)), dma((NS,)), dma((NS,)), dma((J,)),
        dma((parts,)), dma((parts,)),
        dma((parts,)), dma((parts,)),
        dma((parts, 2)), dma((parts, 2)),
        dma((J, 2)), dma((J, 2)),
        dma((J,)), dma((J,)),
        dma((J,)), dma((J,)),
    ]
    any_spec = pl.BlockSpec(memory_space=pl.ANY)
    vmem = pl.BlockSpec(memory_space=pltpu.VMEM)
    flops = 6 * n_exp * rows * D * FFl
    return pl.pallas_call(
        functools.partial(kernel, cfg),
        out_shape=jax.ShapeDtypeStruct((T, D), F32),
        in_specs=[any_spec] * 6,
        out_specs=vmem,
        scratch_shapes=scratch,
        cost_estimate=pl.CostEstimate(flops=flops, bytes_accessed=6 * D * FFl, transcendentals=0),
        compiler_params=pltpu.CompilerParams(
            collective_id=0, has_side_effects=True, vmem_limit_bytes=63 * 1024 * 1024),
    )(tokens, routing, mix_weights, gate_weight, up_weight, down_weight).astype(BF16)


def solution(mesh):
    in_specs = (
        P(("expert", "hidden"), None),
        P(("expert", "hidden"), None),
        P(("expert", "hidden"), None),
        P("expert", None, "hidden"),
        P("expert", None, "hidden"),
        P("expert", "hidden", None),
    )
    out_specs = P(("expert", "hidden"), None)
    return jax.shard_map(shards, mesh=mesh, in_specs=in_specs, out_specs=out_specs, check_vma=False)
```
